32 devices in a mesh: chan: 8 (over z, y), orb: 4 (over x, core).
Axes of the slice: x: 2, y: 2, z: 4, core: 2. Of those that a mesh axis runs over, the one named last changes fastest.
Arguments:
- amplitudes: bfloat16 [20480, 1024], P(('chan', 'orb')), may hold values from -6 to 6
- recoupling: float32 [20480], P(('chan', 'orb')), may hold values from -1.5 to 1.5
- denominators: float32 [20480], P(('chan', 'orb')), may hold values from 1 to 8
- interaction: bfloat16 [32, 1024, 1024], P('chan', 'orb'), may hold values from -0.25 to 0.25
- pair_source: int32 [32, 1024], P('chan', 'orb'), may hold values from -1 to 639, as said below
- return_slot: int32 [20480], P(('chan', 'orb')), may hold values from 0 to 1023, as said below
- channel_sizes: int32 [32], P('chan'), may hold values from 256 to 1024, as said below
Outputs:
- updated: bfloat16 [20480, 1024], P(('chan', 'orb'))
The draws below stay inside these ranges and needn't reach their ends.
Inputs may be any that keep to these rules, and one draw needn't show every extreme that they name: `channel_sizes`: every channel size is a multiple of 4; the 4 sizes of blocks c with the same c div 4 sum to 2560. pair_source[c, p] = -1 exactly where live[c, p] = 0. For each e and o, over the blocks c with c div 4 = e and the positions p with p div 256 = o, the other values name each number 0 to 639 once. return_slot[(e * 4 + o) * 640 + i] is the k with pair_source[e * 4 + k div 256, o * 256 + k mod 256] = i.
All inputs are finite; a program needn't handle non-finite values.
Results may differ from the reference program's by a relative error of at most 0.002.
Values may be sent and summed in bfloat16 or wider, within the bound.
A program may use at most 64 MiB of HBM per device.

```python
import math
import jax
import jax.numpy as jnp
from jax import lax

B = 1024
BLK_DEV = 4
MEAN_SIZE = 640
ROWS_BLOCK = 256
P_DEV = 640
QUOTA = 80
NB = 32
PP_ROWS = 20480
N_CHAN = 8
N_ORB = 4


def layout(key):
    size_key, perm_key = jax.random.split(jax.random.fold_in(key, 11))
    chan_total = NB // BLK_DEV
    orb_total = B // ROWS_BLOCK
    spread = (B - MEAN_SIZE) // orb_total
    half_shift = jax.random.randint(size_key, (chan_total, BLK_DEV // 2), -spread, spread + 1)
    half_shift = half_shift.at[0, 0].set(spread)
    half_shift = half_shift.at[0, BLK_DEV // 2 - 1].set(-spread)
    block_sizes = jnp.stack([MEAN_SIZE + orb_total * half_shift, MEAN_SIZE - orb_total * half_shift], axis=2)
    block_sizes = block_sizes.reshape(chan_total, BLK_DEV).astype(jnp.int32)
    column_ids = jnp.arange(ROWS_BLOCK, dtype=jnp.int32)
    orb_ids = jnp.arange(orb_total, dtype=jnp.int32)
    pair_rank = orb_total * column_ids[None, :] + orb_ids[:, None]
    live_mask = pair_rank[None, :, None, :] < block_sizes[:, None, :, None]
    live_flat = live_mask.reshape(chan_total, orb_total, BLK_DEV * ROWS_BLOCK)
    live_order = jnp.cumsum(live_flat.astype(jnp.int32), axis=2) - 1
    perm_keys = jax.random.split(perm_key, chan_total * orb_total)
    shuffles = jax.vmap(lambda subkey: jax.random.permutation(subkey, P_DEV))(perm_keys)
    shuffles = shuffles.reshape(chan_total, orb_total, P_DEV).astype(jnp.int32)
    picked = jnp.take_along_axis(shuffles, jnp.clip(live_order, 0, P_DEV - 1), axis=2)
    source = jnp.where(live_flat, picked, -1).astype(jnp.int32)
    pair_source = source.reshape(chan_total, orb_total, BLK_DEV, ROWS_BLOCK).transpose(0, 2, 1, 3).reshape(NB, B)
    local_ids = jnp.arange(BLK_DEV * ROWS_BLOCK, dtype=jnp.int32)
    sort_score = jnp.where(live_flat, source, P_DEV + local_ids[None, None, :])
    return_slot = jnp.argsort(sort_score, axis=2, stable=True)[:, :, :P_DEV].reshape(-1).astype(jnp.int32)
    return (block_sizes.reshape(NB), pair_source, return_slot)


def draw_channel_sizes(key, part):
    return layout(key)[0]


def draw_pair_source(key, part):
    return layout(key)[1]


def draw_return_slot(key, part):
    return layout(key)[2]


def block_scale(own_key, extent, shards, least, top_value):
    loudness = 1.0
    for dim, shards_of in shards:
        draws = jax.random.uniform(jax.random.fold_in(jax.random.fold_in(own_key, 6), dim), (shards_of,), jnp.float32, least / len(shards), top_value / len(shards))
        loudness = loudness * jnp.repeat(jnp.exp(draws), extent[dim] // shards_of).reshape((-1,) + (1,) * (len(extent) - 1 - dim))
    return loudness


def normal_values(stream_key, dims, width, most, pieces=(), kind=jnp.bfloat16):
    drawn = jax.random.normal(stream_key, dims, jnp.float32) * width
    if len(pieces) > 0:
        drawn = block_scale(stream_key, dims, pieces, -0.22, 0.18) * drawn
    return jnp.clip(drawn, min=-most, max=most).astype(kind)


def setup_inputs(seed: int = 0) -> dict:
    keys = jax.random.split(jax.random.key(seed), 8)
    return {
        "amplitudes": normal_values(keys[0], (PP_ROWS, B), 1.0, 6.0, ((0, 32),)),
        "recoupling": jnp.clip(jax.random.uniform(keys[1], (PP_ROWS,), jnp.float32, -1.5, 1.5) * block_scale(keys[1], (PP_ROWS,), ((0, 32),), -0.4, 0.0), -1.5, 1.5),
        "denominators": jnp.clip(jnp.exp(math.log(8.0) - 2.0794415 * jax.random.uniform(keys[2], (PP_ROWS,), jnp.float32) ** block_scale(keys[2], (PP_ROWS,), ((0, 32),), -0.2, 0.2)), 1.0, 8.0),
        "interaction": normal_values(keys[3], (NB, B, B), MEAN_SIZE ** -0.5, 0.25, ((0, 8), (1, 4))),
        "pair_source": draw_pair_source(jax.random.fold_in(keys[7], 71), 0),
        "return_slot": draw_return_slot(jax.random.fold_in(keys[7], 71), 0),
        "channel_sizes": draw_channel_sizes(jax.random.fold_in(keys[7], 71), 0),
    }


def reference(amplitudes, recoupling, denominators, interaction, pair_source, return_slot, channel_sizes):
    amp_grid = amplitudes.reshape(N_CHAN, N_ORB, P_DEV, B)
    weight_grid = recoupling.reshape(N_CHAN, N_ORB, P_DEV)
    slot_grid = return_slot.reshape(N_CHAN, N_ORB, P_DEV)
    position = jnp.arange(B, dtype=jnp.int32)
    pair_rank = N_ORB * (position % ROWS_BLOCK) + position // ROWS_BLOCK
    owner_orb = position // ROWS_BLOCK
    orb_ids = jnp.arange(N_ORB, dtype=jnp.int32)

    def per_chan(chan_number):
        offset = (chan_number * QUOTA).astype(jnp.int32)
        sent_amp = lax.dynamic_slice_in_dim(amp_grid, offset, QUOTA, 2)
        sent_weight = lax.dynamic_slice_in_dim(weight_grid, offset, QUOTA, 2)
        relayed = (sent_amp.astype(jnp.float32) * sent_weight[..., None]).astype(jnp.bfloat16)
        received = jnp.transpose(relayed, (1, 0, 2, 3)).reshape(N_ORB * P_DEV, B)
        first_block = (chan_number * BLK_DEV).astype(jnp.int32)
        source = lax.dynamic_slice_in_dim(pair_source, first_block, BLK_DEV, 0)
        block_sizes = lax.dynamic_slice_in_dim(channel_sizes, first_block, BLK_DEV, 0)
        gather_at = owner_orb[None, :] * P_DEV + jnp.maximum(source, 0)
        amp_block = jnp.take(received, gather_at.reshape(-1), axis=0).reshape(BLK_DEV, B, B)
        live_mask = pair_rank[None, :] < block_sizes[:, None]
        keep = (source >= 0)[:, :, None] & live_mask[:, None, :]
        amp_block = jnp.where(keep, amp_block, jnp.zeros((), amp_block.dtype))
        weights_block = lax.dynamic_slice_in_dim(interaction, first_block, BLK_DEV, 0)
        cycle_block = jnp.einsum("bik,bkj->bij", weights_block.astype(jnp.float32), amp_block.astype(jnp.float32)).astype(jnp.bfloat16)
        local_rows = lax.dynamic_slice_in_dim(slot_grid, chan_number.astype(jnp.int32), 1, 0)[0]
        block_id = local_rows // ROWS_BLOCK
        row_pos = orb_ids[:, None] * ROWS_BLOCK + local_rows % ROWS_BLOCK
        flat_rows = (block_id * B + row_pos).reshape(-1)
        picked = jnp.take(cycle_block.reshape(BLK_DEV * B, B), flat_rows, axis=0)
        return picked.reshape(N_ORB, P_DEV, B)

    returned = lax.map(per_chan, jnp.arange(N_CHAN, dtype=jnp.int32))
    returned = returned.reshape(N_CHAN, N_ORB, N_CHAN, QUOTA, B).transpose(2, 1, 0, 3, 4)
    returned = returned.reshape(N_CHAN, N_ORB * P_DEV, B)

    def finish(packed):
        amp_rows, cycle_rows, weight_rows, denom_rows = packed
        total = amp_rows.astype(jnp.float32) + (weight_rows[:, None] * cycle_rows.astype(jnp.float32)) / denom_rows[:, None]
        return total.astype(jnp.bfloat16)

    updated = lax.map(finish, (amplitudes.reshape(N_CHAN, N_ORB * P_DEV, B), returned, recoupling.reshape(N_CHAN, N_ORB * P_DEV), denominators.reshape(N_CHAN, N_ORB * P_DEV)))
    return updated.reshape(PP_ROWS, B)
```

```python
import functools

import jax
import jax.numpy as jnp
from jax import lax
from jax.experimental import pallas as pl
from jax.experimental.pallas import tpu as pltpu
from jax.sharding import PartitionSpec as P

MESH = pl.DeviceIdType.MESH


def peer_of(index, step, count):
    total, bit = 0, 1
    while bit < count:
        digit = lax.rem(lax.div(index, bit), 2)
        total = total + lax.rem(digit + (step // bit) % 2, 2) * bit
        bit *= 2
    return total


def step_order(count):
    steps = list(range(1, count))
    far = [s for s in steps if s >= count // 2]
    near = [s for s in steps if 1 < s < count // 2]
    first = [s for s in steps if s == 1 and s < count // 2]
    return first + far + near


def kernel(
    n_chan, n_orb, amp_ref, rec_ref, ps_ref, size_ref, w_ref, out_ref,
    send_buf, recv_buf, ps_all, w_buf, mix, hot, picked, row_block, row_size, back_buf,
    w_sem, ps_send, ps_recv, go_send, go_recv, cross_send, core_send, back_send, back_recv,
):
    e = lax.axis_index("chan")
    o = lax.axis_index("orb")
    quota, width = send_buf.shape[1:]
    rows = n_chan * quota
    blocks, rows_block = w_buf.shape[:2]
    local = blocks * rows_block
    pairs = n_orb // 2
    core = lax.rem(o, 2)
    pair = lax.div(o, 2)
    mate = o + 1 - 2 * core
    tile = 2 * quota
    order = step_order(n_chan)

    w_copy = pltpu.make_async_copy(w_ref, w_buf, w_sem)
    w_copy.start()

    barrier = pltpu.get_barrier_semaphore()
    for step in range(1, n_chan):
        pl.semaphore_signal(
            barrier, inc=1, device_id=(peer_of(e, step, n_chan), o), device_id_type=MESH
        )
    for step in range(1, n_orb):
        pl.semaphore_signal(
            barrier, inc=1, device_id=(e, lax.rem(o + step, n_orb)), device_id_type=MESH
        )

    def relay(d):
        at = pl.ds(pl.multiple_of(d * quota, quota), quota)
        return (amp_ref[at, :].astype(jnp.float32) * rec_ref[at, :]).astype(jnp.bfloat16)

    recv_buf[o, e] = relay(e)

    def fill(d, carry):
        send_buf[d] = relay(d)
        return carry

    lax.fori_loop(0, n_chan, fill, 0)
    ps_all[o] = ps_ref[...]
    pl.semaphore_wait(barrier, n_chan + n_orb - 2)

    def go(step):
        d = peer_of(e, step, n_chan)
        return pltpu.make_async_remote_copy(
            src_ref=send_buf.at[d], dst_ref=recv_buf.at[o, e],
            send_sem=go_send.at[d], recv_sem=go_recv.at[o, e],
            device_id=(d, o), device_id_type=MESH,
        )

    def slot_copy(s, d, sem, target):
        return pltpu.make_async_remote_copy(
            src_ref=recv_buf.at[s, d], dst_ref=recv_buf.at[s, d],
            send_sem=sem, recv_sem=go_recv.at[s, d],
            device_id=(e, target), device_id_type=MESH,
        )

    def ps_copy(step):
        target = lax.rem(o + step, n_orb)
        return pltpu.make_async_remote_copy(
            src_ref=ps_all.at[o], dst_ref=ps_all.at[o],
            send_sem=ps_send.at[step], recv_sem=ps_recv.at[o],
            device_id=(e, target), device_id_type=MESH,
        )

    def ps_wait(step):
        s = lax.rem(o + step, n_orb)
        pltpu.make_async_remote_copy(
            src_ref=ps_all.at[s], dst_ref=ps_all.at[s],
            send_sem=ps_send.at[step], recv_sem=ps_recv.at[s],
            device_id=(e, s), device_id_type=MESH,
        ).wait_recv()

    started = []

    def launch(copy):
        copy.start()
        started.append(copy)

    def spread(d):
        for j in range(1, pairs):
            target = lax.rem(pair + j, pairs) * 2 + core
            launch(slot_copy(o, d, cross_send.at[j, d], target))
        launch(slot_copy(o, d, core_send.at[0, d], mate))

    def pass_on(d):
        for j in range(1, pairs):
            s = lax.rem(pair + j, pairs) * 2 + core
            slot_copy(s, d, core_send.at[j, d], mate).wait_recv()
            launch(slot_copy(s, d, core_send.at[j, d], mate))

    for step in order:
        launch(go(step))
    spread(e)
    for step in range(1, n_orb):
        launch(ps_copy(step))

    def pick_rows(t):
        if t == 0:
            w_copy.wait()
        base = t * tile
        own = ps_all[o][0:1, :]
        rank = lax.broadcasted_iota(jnp.int32, (tile, local), 0) + base
        hit = rank == own
        lane_block = lax.broadcasted_iota(jnp.int32, (tile, local), 1) // rows_block
        row_block[base:base + tile, :] = jnp.broadcast_to(
            jnp.sum(jnp.where(hit, lane_block, 0).astype(jnp.float32), axis=1, keepdims=True), (tile, 128)
        )
        row_size[base:base + tile, :] = jnp.broadcast_to(
            jnp.sum(jnp.where(hit, size_ref[0:1, :], 0).astype(jnp.float32), axis=1, keepdims=True), (tile, 128)
        )
        chosen = jnp.where(hit, 1.0, 0.0).astype(jnp.bfloat16)
        total = None
        for c in range(blocks):
            term = jnp.dot(
                chosen[:, c * rows_block:(c + 1) * rows_block], w_buf[c],
                preferred_element_type=jnp.float32,
            )
            total = term if total is None else total + term
        picked[base:base + tile, :] = total.astype(jnp.bfloat16)

    def mix_columns(step):
        s = lax.rem(o + step, n_orb)
        if step > 0:
            ps_wait(step)
        source = ps_all[s][0:1, :]

        def heat(t, carry):
            at = pl.ds(pl.multiple_of(t * quota, quota), quota)
            rank = lax.broadcasted_iota(jnp.int32, (quota, local), 0) + t * quota
            hot[at, :] = jnp.where(rank == source, 1.0, 0.0).astype(jnp.bfloat16)
            return carry

        lax.fori_loop(0, n_chan, heat, 0)

        def part(t, carry):
            at = pl.ds(pl.multiple_of(t * tile, tile), tile)
            mine = picked[at, pl.ds(pl.multiple_of(s * rows_block, rows_block), rows_block)].astype(jnp.float32)
            which = row_block[at, 0:1]
            total = None
            for c in range(blocks):
                left = jnp.where(which == c, mine, 0.0).astype(jnp.bfloat16)
                term = lax.dot_general(
                    left, hot[:, c * rows_block:(c + 1) * rows_block],
                    (((1,), (1,)), ((), ())), preferred_element_type=jnp.float32,
                )
                total = term if total is None else total + term
            mix[s, at, :] = total.astype(jnp.bfloat16)
            return carry

        lax.fori_loop(0, rows // tile, part, 0)

    pieces = [functools.partial(pick_rows, t) for t in range(rows // tile)]
    pieces += [functools.partial(mix_columns, s) for s in range(n_orb)]
    arrivals = [peer_of(e, step, n_chan) for step in order]
    known = [e]
    for k in range(max(len(pieces), len(arrivals))):
        if k < len(pieces):
            pieces[k]()
        if k < len(arrivals):
            d = arrivals[k]
            slot_copy(o, d, core_send.at[0, d], mate).wait_recv()
            spread(d)
            pass_on(known[-1])
            known.append(d)
    pass_on(known[-1])
    for d in known:
        for j in range(pairs):
            s = lax.rem(pair + j, pairs) * 2 + (1 - core)
            slot_copy(s, d, core_send.at[j, d], mate).wait_recv()

    half = n_chan // 2
    columns = 256

    def back(d):
        return pltpu.make_async_remote_copy(
            src_ref=back_buf.at[d], dst_ref=out_ref.at[e],
            send_sem=back_send.at[d], recv_sem=back_recv.at[e],
            device_id=(d, o), device_id_type=MESH,
        )

    for g in range(half):
        first = lax.rem(lax.div(e, 2) + half // 2 + g, half) * 2
        at = pl.ds(pl.multiple_of(first * quota, tile), tile)

        def product(n, carry):
            cols = pl.ds(pl.multiple_of(n * columns, columns), columns)
            total = None
            for s in range(n_orb):
                term = jnp.dot(
                    mix[s, at, :], recv_buf[s, :, :, cols].reshape(rows, columns),
                    preferred_element_type=jnp.float32,
                )
                total = term if total is None else total + term
            k = lax.broadcasted_iota(jnp.int32, (tile, columns), 1) + n * columns
            rank = n_orb * lax.rem(k, rows_block) + lax.div(k, rows_block)
            kept = jnp.where(rank.astype(jnp.float32) < row_size[at, 0:1], total, 0.0)
            back_buf[pl.ds(first, 2), :, cols] = kept.astype(jnp.bfloat16).reshape(2, quota, columns)
            return carry

        lax.fori_loop(0, width // columns, product, 0)
        for i in range(2):
            if g == half // 2:
                continue
            launch(back(first + i))
        if g == half // 2:
            launch(back(peer_of(e, 1, n_chan)))
            out_ref[e] = back_buf[e]

    for step in range(1, n_chan):
        d = peer_of(e, step, n_chan)
        pltpu.make_async_remote_copy(
            src_ref=back_buf.at[d], dst_ref=out_ref.at[d],
            send_sem=back_send.at[d], recv_sem=back_recv.at[d],
            device_id=(d, o), device_id_type=MESH,
        ).wait_recv()
    for copy in started:
        copy.wait_send()


def fused(amplitudes, recoupling, interaction, pair_source, channel_sizes):
    n_chan, n_orb = lax.axis_size("chan"), lax.axis_size("orb")
    rows, width = amplitudes.shape
    quota = rows // n_chan
    blocks, rows_block = pair_source.shape
    local = blocks * rows_block
    bf16, f32 = jnp.bfloat16, jnp.float32
    vmem = pl.BlockSpec(memory_space=pltpu.VMEM)
    dma = pltpu.SemaphoreType.DMA
    source = jnp.broadcast_to(pair_source.reshape(1, local), (8, local))
    sizes = jnp.broadcast_to(jnp.repeat(channel_sizes, rows_block)[None, :], (8, local))
    out = pl.pallas_call(
        functools.partial(kernel, n_chan, n_orb),
        out_shape=jax.ShapeDtypeStruct((n_chan, quota, width), bf16),
        in_specs=[vmem] * 4 + [pl.BlockSpec(memory_space=pl.ANY)],
        out_specs=vmem,
        scratch_shapes=[
            pltpu.VMEM((n_chan, quota, width), bf16),
            pltpu.VMEM((n_orb, n_chan, quota, width), bf16),
            pltpu.VMEM((n_orb, 8, local), jnp.int32),
            pltpu.VMEM(interaction.shape, bf16),
            pltpu.VMEM((n_orb, rows, rows), bf16),
            pltpu.VMEM((rows, local), bf16),
            pltpu.VMEM((rows, width), bf16),
            pltpu.VMEM((rows, 128), f32),
            pltpu.VMEM((rows, 128), f32),
            pltpu.VMEM((n_chan, quota, width), bf16),
            dma,
            dma((n_orb,)),
            dma((n_orb,)),
            dma((n_chan,)),
            dma((n_orb, n_chan)),
            dma((n_orb // 2, n_chan)),
            dma((n_orb // 2, n_chan)),
            dma((n_chan,)),
            dma((n_chan,)),
        ],
        compiler_params=pltpu.CompilerParams(
            collective_id=0, has_side_effects=True, vmem_limit_bytes=48 * 1024 * 1024
        ),
        name="cycle",
    )(amplitudes, recoupling[:, None], source, sizes, interaction)
    return out.reshape(rows, width)


def exchanged(amplitudes, recoupling, interaction, pair_source, return_slot, channel_sizes):
    chan_count = lax.axis_size("chan")
    orb_count = lax.axis_size("orb")
    row_count = amplitudes.shape[0]
    width = amplitudes.shape[1]
    per_peer = row_count // chan_count
    blocks_here = pair_source.shape[0]
    rows_block = pair_source.shape[1]
    relayed = (amplitudes.astype(jnp.float32) * recoupling[:, None]).astype(jnp.bfloat16)
    received = lax.all_to_all(
        relayed.reshape(chan_count, per_peer, width),
        "chan",
        split_axis=0,
        concat_axis=0,
        tiled=True,
    )
    received = received.reshape(row_count, width)
    flat_source = pair_source.reshape(-1)
    amp_rows = jnp.take(received, jnp.maximum(flat_source, 0), axis=0)
    position = jnp.arange(width, dtype=jnp.int32)
    pair_rank = orb_count * (position % rows_block) + position // rows_block
    live_mask = pair_rank[None, :] < channel_sizes[:, None]
    keep = (pair_source >= 0)[:, :, None] & live_mask[:, None, :]
    amp_block = jnp.where(
        keep, amp_rows.reshape(blocks_here, rows_block, width), jnp.zeros((), jnp.bfloat16)
    )
    cycle_local = jnp.einsum(
        "bik,bkj->bij",
        interaction,
        lax.all_gather(amp_block, "orb", axis=1, tiled=True),
        preferred_element_type=jnp.float32,
    ).astype(jnp.bfloat16)
    outgoing = jnp.take(cycle_local.reshape(blocks_here * rows_block, width), return_slot, axis=0)
    returned = lax.all_to_all(
        outgoing.reshape(chan_count, per_peer, width),
        "chan",
        split_axis=0,
        concat_axis=0,
        tiled=True,
    )
    returned = returned.reshape(row_count, width)
    return returned


def fits(amplitudes, pair_source):
    n_chan, n_orb = lax.axis_size("chan"), lax.axis_size("orb")
    rows, width = amplitudes.shape
    quota = rows // n_chan
    rows_block = pair_source.shape[1]
    return (
        quota % 16 == 0 and rows % 128 == 0 and n_chan % 4 == 0 and n_chan & (n_chan - 1) == 0
        and n_orb % 2 == 0 and rows_block % 128 == 0 and width % 256 == 0 and n_chan <= 16
    )


def shards(
    amplitudes, recoupling, denominators, interaction, pair_source, return_slot, channel_sizes
):
    if fits(amplitudes, pair_source):
        returned = fused(amplitudes, recoupling, interaction, pair_source, channel_sizes)
    else:
        returned = exchanged(
            amplitudes, recoupling, interaction, pair_source, return_slot, channel_sizes
        )
    updated = (
        amplitudes.astype(jnp.float32)
        + recoupling[:, None] * returned.astype(jnp.float32) / denominators[:, None]
    )
    return updated.astype(jnp.bfloat16)


def solution(mesh):
    in_specs = (
        P(("chan", "orb"), None),
        P(("chan", "orb")),
        P(("chan", "orb")),
        P("chan", "orb", None),
        P("chan", "orb"),
        P(("chan", "orb")),
        P("chan"),
    )
    out_specs = P(("chan", "orb"), None)
    return jax.shard_map(shards, mesh=mesh, in_specs=in_specs, out_specs=out_specs, check_vma=False)
```

```python
import functools

import jax
import jax.numpy as jnp
from jax import lax
from jax.experimental import pallas as pl
from jax.experimental.pallas import tpu as pltpu
from jax.sharding import PartitionSpec as P

MESH = pl.DeviceIdType.MESH


def peer_of(index, step, count):
    total, bit = 0, 1
    while bit < count:
        digit = lax.rem(lax.div(index, bit), 2)
        total = total + lax.rem(digit + (step // bit) % 2, 2) * bit
        bit *= 2
    return total


def kernel(
    n_chan, n_orb, amp_ref, rec_ref, ps_ref, size_ref, w_ref, out_ref,
    amp_buf, weight, total_buf, send_buf, recv_buf, ps_all, w_buf, mix, hot, picked, row_block,
    row_size, back_buf, amp_sem, w_sem, ps_send, ps_recv, go_send, go_recv, cross_send, core_send, back_send, back_recv,
):
    e = lax.axis_index("chan")
    o = lax.axis_index("orb")
    quota, width = send_buf.shape[1:]
    rows = n_chan * quota
    blocks, rows_block = w_buf.shape[:2]
    local = blocks * rows_block
    pairs = n_orb // 2
    core = lax.rem(o, 2)
    pair = lax.div(o, 2)
    mate = o + 1 - 2 * core
    tile = 2 * quota
    half = n_chan // 2
    order = list(range(1, n_chan))

    amp_copy = pltpu.make_async_copy(amp_ref, amp_buf, amp_sem)
    amp_copy.start()
    w_copy = pltpu.make_async_copy(w_ref, w_buf, w_sem)
    w_copy.start()

    barrier = pltpu.get_barrier_semaphore()
    for step in range(1, n_chan):
        pl.semaphore_signal(
            barrier, inc=1, device_id=(peer_of(e, step, n_chan), o), device_id_type=MESH
        )
    for step in range(1, n_orb):
        pl.semaphore_signal(
            barrier, inc=1, device_id=(e, lax.rem(o + step, n_orb)), device_id_type=MESH
        )

    def relay(d):
        at = pl.ds(pl.multiple_of(d * quota, quota), quota)
        return (amp_buf[at, :].astype(jnp.float32) * weight[at, 0:1]).astype(jnp.bfloat16)

    weight[...] = jnp.broadcast_to(rec_ref[0:1, :], (128, rows)).T
    ps_all[o] = ps_ref[...]
    amp_copy.wait()
    recv_buf[o, e] = relay(e)
    pl.semaphore_wait(barrier, n_chan + n_orb - 2)

    def go(step):
        d = peer_of(e, step, n_chan)
        return pltpu.make_async_remote_copy(
            src_ref=send_buf.at[d], dst_ref=recv_buf.at[o, e],
            send_sem=go_send.at[d], recv_sem=go_recv.at[o, e],
            device_id=(d, o), device_id_type=MESH,
        )

    def slot_copy(s, d, sem, target):
        return pltpu.make_async_remote_copy(
            src_ref=recv_buf.at[s, d], dst_ref=recv_buf.at[s, d],
            send_sem=sem, recv_sem=go_recv.at[s, d],
            device_id=(e, target), device_id_type=MESH,
        )

    def ps_copy(step):
        target = lax.rem(o + step, n_orb)
        return pltpu.make_async_remote_copy(
            src_ref=ps_all.at[o], dst_ref=ps_all.at[o],
            send_sem=ps_send.at[step], recv_sem=ps_recv.at[o],
            device_id=(e, target), device_id_type=MESH,
        )

    def ps_wait(step):
        s = lax.rem(o + step, n_orb)
        pltpu.make_async_remote_copy(
            src_ref=ps_all.at[s], dst_ref=ps_all.at[s],
            send_sem=ps_send.at[step], recv_sem=ps_recv.at[s],
            device_id=(e, s), device_id_type=MESH,
        ).wait_recv()

    started = []

    def launch(copy):
        copy.start()
        started.append(copy)

    def spread(d):
        for j in range(1, pairs):
            target = lax.rem(pair + j, pairs) * 2 + core
            launch(slot_copy(o, d, cross_send.at[j, d], target))
        launch(slot_copy(o, d, core_send.at[0, d], mate))

    def pass_on(d):
        for j in range(1, pairs):
            s = lax.rem(pair + j, pairs) * 2 + core
            slot_copy(s, d, core_send.at[j, d], mate).wait_recv()
            launch(slot_copy(s, d, core_send.at[j, d], mate))

    spread(e)
    for step in order:
        d = peer_of(e, step, n_chan)
        send_buf[d] = relay(d)
        launch(go(step))
    for step in range(1, n_orb):
        launch(ps_copy(step))

    def pick_rows(t):
        if t == 0:
            w_copy.wait()
        base = t * tile
        own = ps_all[o][0:1, :]
        rank = lax.broadcasted_iota(jnp.int32, (tile, local), 0) + base
        hit = rank == own
        lane_block = lax.broadcasted_iota(jnp.int32, (tile, local), 1) // rows_block
        row_block[base:base + tile, :] = jnp.broadcast_to(
            jnp.sum(jnp.where(hit, lane_block, 0).astype(jnp.float32), axis=1, keepdims=True), (tile, 128)
        )
        row_size[base:base + tile, :] = jnp.broadcast_to(
            jnp.sum(jnp.where(hit, size_ref[0:1, :], 0).astype(jnp.float32), axis=1, keepdims=True), (tile, 128)
        )
        chosen = jnp.where(hit, 1.0, 0.0).astype(jnp.bfloat16)
        total = None
        for c in range(blocks):
            term = jnp.dot(
                chosen[:, c * rows_block:(c + 1) * rows_block], w_buf[c],
                preferred_element_type=jnp.float32,
            )
            total = term if total is None else total + term
        picked[base:base + tile, :] = total.astype(jnp.bfloat16)

    def mix_columns(step):
        s = lax.rem(o + step, n_orb)
        if step > 0:
            ps_wait(step)
        source = ps_all[s][0:1, :]

        def heat(t, carry):
            at = pl.ds(pl.multiple_of(t * quota, quota), quota)
            rank = lax.broadcasted_iota(jnp.int32, (quota, local), 0) + t * quota
            hot[at, :] = jnp.where(rank == source, 1.0, 0.0).astype(jnp.bfloat16)
            return carry

        lax.fori_loop(0, n_chan, heat, 0)

        def part(t, carry):
            at = pl.ds(pl.multiple_of(t * tile, tile), tile)
            mine = picked[at, pl.ds(pl.multiple_of(s * rows_block, rows_block), rows_block)].astype(jnp.float32)
            which = row_block[at, 0:1]
            lefts = [jnp.where(which == c, mine, 0.0).astype(jnp.bfloat16) for c in range(blocks)]
            for h in range(half):
                total = None
                for c in range(blocks):
                    term = lax.dot_general(
                        lefts[c],
                        hot[h * tile:(h + 1) * tile, c * rows_block:(c + 1) * rows_block],
                        (((1,), (1,)), ((), ())), preferred_element_type=jnp.float32,
                    )
                    total = term if total is None else total + term
                mix[s, h, at, :] = total.astype(jnp.bfloat16)
            return carry

        lax.fori_loop(0, rows // tile, part, 0)

    columns = 256
    here = lax.div(e, 2)

    def slab(group, at, cols):
        z = peer_of(here, group, half)
        total = None
        for s in range(n_orb):
            term = jnp.dot(
                mix[s, z, at, :],
                recv_buf[s, pl.ds(2 * z, 2), :, cols].reshape(tile, columns),
                preferred_element_type=jnp.float32,
            )
            total = term if total is None else total + term
        return total

    def gather_group(group):
        for i in range(2):
            d = peer_of(e, 2 * group + i, n_chan)
            for j in range(pairs):
                s = lax.rem(pair + j, pairs) * 2 + (1 - core)
                slot_copy(s, d, core_send.at[j, d], mate).wait_recv()

    def add_groups(groups, fresh):
        for group in groups:
            gather_group(group)

        def block_of(t, carry):
            at = pl.ds(pl.multiple_of(lax.div(t, width // columns) * tile, tile), tile)
            cols = pl.ds(
                pl.multiple_of(lax.rem(t, width // columns) * columns, columns), columns
            )
            total = None if fresh else total_buf[at, cols]
            for group in groups:
                term = slab(group, at, cols)
                total = term if total is None else total + term
            total_buf[at, cols] = total
            return carry

        lax.fori_loop(0, half * (width // columns), block_of, 0)

    near = list(range(half // 2))
    middle = list(range(half // 2, half - 1))
    last = half - 1
    stages = {k: [] for k in range(1, n_chan)}
    stages[1] += [functools.partial(pick_rows, t) for t in range(half)]
    for s in range(n_orb):
        stages[min(2 + s, n_chan - 1)].append(functools.partial(mix_columns, s))
    stages[n_chan - 1].append(functools.partial(add_groups, near, True))
    previous = e
    for step in order:
        for piece in stages[step]:
            piece()
        d = peer_of(e, step, n_chan)
        slot_copy(o, d, core_send.at[0, d], mate).wait_recv()
        spread(d)
        pass_on(previous)
        previous = d
    if middle:
        add_groups(middle, False)
    pass_on(previous)
    gather_group(last)

    def back(d):
        return pltpu.make_async_remote_copy(
            src_ref=back_buf.at[d], dst_ref=out_ref.at[e],
            send_sem=back_send.at[d], recv_sem=back_recv.at[e],
            device_id=(d, o), device_id_type=MESH,
        )

    for g in range(half):
        first = lax.rem(lax.div(e, 2) + half // 2 + g, half) * 2
        at = pl.ds(pl.multiple_of(first * quota, tile), tile)

        def product(n, carry):
            cols = pl.ds(pl.multiple_of(n * columns, columns), columns)
            total = total_buf[at, cols] + slab(last, at, cols)
            k = lax.broadcasted_iota(jnp.int32, (tile, columns), 1) + n * columns
            rank = n_orb * lax.rem(k, rows_block) + lax.div(k, rows_block)
            kept = jnp.where(rank.astype(jnp.float32) < row_size[at, 0:1], total, 0.0)
            back_buf[pl.ds(first, 2), :, cols] = kept.astype(jnp.bfloat16).reshape(2, quota, columns)
            return carry

        lax.fori_loop(0, width // columns, product, 0)
        for i in range(2):
            if g == half // 2:
                continue
            launch(back(first + i))
        if g == half // 2:
            launch(back(peer_of(e, 1, n_chan)))
            out_ref[e] = back_buf[e]

    for step in range(1, n_chan):
        d = peer_of(e, step, n_chan)
        pltpu.make_async_remote_copy(
            src_ref=back_buf.at[d], dst_ref=out_ref.at[d],
            send_sem=back_send.at[d], recv_sem=back_recv.at[d],
            device_id=(d, o), device_id_type=MESH,
        ).wait_recv()
    for copy in started:
        copy.wait_send()


def fused(amplitudes, recoupling, interaction, pair_source, channel_sizes):
    n_chan, n_orb = lax.axis_size("chan"), lax.axis_size("orb")
    rows, width = amplitudes.shape
    quota = rows // n_chan
    blocks, rows_block = pair_source.shape
    local = blocks * rows_block
    bf16, f32 = jnp.bfloat16, jnp.float32
    vmem = pl.BlockSpec(memory_space=pltpu.VMEM)
    hbm = pl.BlockSpec(memory_space=pltpu.HBM)
    dma = pltpu.SemaphoreType.DMA
    weights = jnp.broadcast_to(recoupling[None, :], (8, rows))
    source = jnp.broadcast_to(pair_source.reshape(1, local), (8, local))
    sizes = jnp.broadcast_to(jnp.repeat(channel_sizes, rows_block)[None, :], (8, local))
    out = pl.pallas_call(
        functools.partial(kernel, n_chan, n_orb),
        out_shape=jax.ShapeDtypeStruct((n_chan, quota, width), bf16),
        in_specs=[hbm] + [vmem] * 3 + [hbm],
        out_specs=vmem,
        scratch_shapes=[
            pltpu.VMEM((rows, width), bf16),
            pltpu.VMEM((rows, 128), f32),
            pltpu.VMEM((rows, width), f32),
            pltpu.VMEM((n_chan, quota, width), bf16),
            pltpu.VMEM((n_orb, n_chan, quota, width), bf16),
            pltpu.VMEM((n_orb, 8, local), jnp.int32),
            pltpu.VMEM(interaction.shape, bf16),
            pltpu.VMEM((n_orb, n_chan // 2, rows, 2 * quota), bf16),
            pltpu.VMEM((rows, local), bf16),
            pltpu.VMEM((rows, width), bf16),
            pltpu.VMEM((rows, 128), f32),
            pltpu.VMEM((rows, 128), f32),
            pltpu.VMEM((n_chan, quota, width), bf16),
            dma,
            dma,
            dma((n_orb,)),
            dma((n_orb,)),
            dma((n_chan,)),
            dma((n_orb, n_chan)),
            dma((n_orb // 2, n_chan)),
            dma((n_orb // 2, n_chan)),
            dma((n_chan,)),
            dma((n_chan,)),
        ],
        compiler_params=pltpu.CompilerParams(
            collective_id=0, has_side_effects=True, vmem_limit_bytes=48 * 1024 * 1024
        ),
        name="cycle",
    )(amplitudes, weights, source, sizes, interaction)
    return out.reshape(rows, width)


def exchanged(amplitudes, recoupling, interaction, pair_source, return_slot, channel_sizes):
    chan_count = lax.axis_size("chan")
    orb_count = lax.axis_size("orb")
    row_count = amplitudes.shape[0]
    width = amplitudes.shape[1]
    per_peer = row_count // chan_count
    blocks_here = pair_source.shape[0]
    rows_block = pair_source.shape[1]
    relayed = (amplitudes.astype(jnp.float32) * recoupling[:, None]).astype(jnp.bfloat16)
    received = lax.all_to_all(
        relayed.reshape(chan_count, per_peer, width),
        "chan",
        split_axis=0,
        concat_axis=0,
        tiled=True,
    )
    received = received.reshape(row_count, width)
    flat_source = pair_source.reshape(-1)
    amp_rows = jnp.take(received, jnp.maximum(flat_source, 0), axis=0)
    position = jnp.arange(width, dtype=jnp.int32)
    pair_rank = orb_count * (position % rows_block) + position // rows_block
    live_mask = pair_rank[None, :] < channel_sizes[:, None]
    keep = (pair_source >= 0)[:, :, None] & live_mask[:, None, :]
    amp_block = jnp.where(
        keep, amp_rows.reshape(blocks_here, rows_block, width), jnp.zeros((), jnp.bfloat16)
    )
    cycle_local = jnp.einsum(
        "bik,bkj->bij",
        interaction,
        lax.all_gather(amp_block, "orb", axis=1, tiled=True),
        preferred_element_type=jnp.float32,
    ).astype(jnp.bfloat16)
    outgoing = jnp.take(cycle_local.reshape(blocks_here * rows_block, width), return_slot, axis=0)
    returned = lax.all_to_all(
        outgoing.reshape(chan_count, per_peer, width),
        "chan",
        split_axis=0,
        concat_axis=0,
        tiled=True,
    )
    returned = returned.reshape(row_count, width)
    return returned


def fits(amplitudes, pair_source):
    n_chan, n_orb = lax.axis_size("chan"), lax.axis_size("orb")
    rows, width = amplitudes.shape
    quota = rows // n_chan
    rows_block = pair_source.shape[1]
    return (
        quota % 16 == 0 and rows % 128 == 0 and n_chan % 4 == 0 and n_chan & (n_chan - 1) == 0
        and n_orb % 2 == 0 and rows_block % 128 == 0 and width % 256 == 0 and n_chan <= 16
    )


def shards(
    amplitudes, recoupling, denominators, interaction, pair_source, return_slot, channel_sizes
):
    if fits(amplitudes, pair_source):
        returned = fused(amplitudes, recoupling, interaction, pair_source, channel_sizes)
    else:
        returned = exchanged(
            amplitudes, recoupling, interaction, pair_source, return_slot, channel_sizes
        )
    updated = (
        amplitudes.astype(jnp.float32)
        + recoupling[:, None] * returned.astype(jnp.float32) / denominators[:, None]
    )
    return updated.astype(jnp.bfloat16)


def solution(mesh):
    in_specs = (
        P(("chan", "orb"), None),
        P(("chan", "orb")),
        P(("chan", "orb")),
        P("chan", "orb", None),
        P("chan", "orb"),
        P(("chan", "orb")),
        P("chan"),
    )
    out_specs = P(("chan", "orb"), None)
    return jax.shard_map(shards, mesh=mesh, in_specs=in_specs, out_specs=out_specs, check_vma=False)
```

```python
import functools

import jax
import jax.numpy as jnp
from jax import lax
from jax.experimental import pallas as pl
from jax.experimental.pallas import tpu as pltpu
from jax.sharding import PartitionSpec as P

MESH = pl.DeviceIdType.MESH


def peer_of(index, step, count):
    total, bit = 0, 1
    while bit < count:
        digit = lax.rem(lax.div(index, bit), 2)
        total = total + lax.rem(digit + (step // bit) % 2, 2) * bit
        bit *= 2
    return total


def kernel(
    n_chan, n_orb, amp_ref, rec_ref, ps_ref, size_ref, w_ref, out_ref,
    amp_buf, weight, total_buf, send_buf, recv_buf, ps_all, w_buf, mix, hot, picked, row_block,
    row_size, back_buf, amp_sem, w_sem, ps_send, ps_recv, go_send, go_recv, cross_send, core_send, back_send, back_recv,
):
    e = lax.axis_index("chan")
    o = lax.axis_index("orb")
    quota, width = send_buf.shape[1:]
    rows = n_chan * quota
    blocks, rows_block = w_buf.shape[:2]
    local = blocks * rows_block
    pairs = n_orb // 2
    core = lax.rem(o, 2)
    pair = lax.div(o, 2)
    mate = o + 1 - 2 * core
    tile = 2 * quota
    half = n_chan // 2
    order = list(range(1, n_chan))

    amp_copy = pltpu.make_async_copy(amp_ref, amp_buf, amp_sem)
    amp_copy.start()
    w_copy = pltpu.make_async_copy(w_ref, w_buf, w_sem)
    w_copy.start()

    barrier = pltpu.get_barrier_semaphore()
    for step in range(1, n_chan):
        pl.semaphore_signal(
            barrier, inc=1, device_id=(peer_of(e, step, n_chan), o), device_id_type=MESH
        )
    for step in range(1, n_orb):
        pl.semaphore_signal(
            barrier, inc=1, device_id=(e, lax.rem(o + step, n_orb)), device_id_type=MESH
        )

    def relay(d):
        at = pl.ds(pl.multiple_of(d * quota, quota), quota)
        return (amp_buf[at, :].astype(jnp.float32) * weight[at, 0:1]).astype(jnp.bfloat16)

    weight[...] = jnp.broadcast_to(rec_ref[0:1, :], (128, rows)).T
    ps_all[o] = ps_ref[...]
    amp_copy.wait()
    recv_buf[o, e] = relay(e)
    pl.semaphore_wait(barrier, n_chan + n_orb - 2)

    def go(step):
        d = peer_of(e, step, n_chan)
        return pltpu.make_async_remote_copy(
            src_ref=send_buf.at[d], dst_ref=recv_buf.at[o, e],
            send_sem=go_send.at[d], recv_sem=go_recv.at[o, e],
            device_id=(d, o), device_id_type=MESH,
        )

    def slot_copy(s, d, sem, target):
        return pltpu.make_async_remote_copy(
            src_ref=recv_buf.at[s, d], dst_ref=recv_buf.at[s, d],
            send_sem=sem, recv_sem=go_recv.at[s, d],
            device_id=(e, target), device_id_type=MESH,
        )

    def ps_copy(step):
        target = lax.rem(o + step, n_orb)
        return pltpu.make_async_remote_copy(
            src_ref=ps_all.at[o], dst_ref=ps_all.at[o],
            send_sem=ps_send.at[step], recv_sem=ps_recv.at[o],
            device_id=(e, target), device_id_type=MESH,
        )

    def ps_wait(step):
        s = lax.rem(o + step, n_orb)
        pltpu.make_async_remote_copy(
            src_ref=ps_all.at[s], dst_ref=ps_all.at[s],
            send_sem=ps_send.at[step], recv_sem=ps_recv.at[s],
            device_id=(e, s), device_id_type=MESH,
        ).wait_recv()

    started = []

    def launch(copy):
        copy.start()
        started.append(copy)

    def spread(d):
        for j in range(1, pairs):
            target = lax.rem(pair + j, pairs) * 2 + core
            launch(slot_copy(o, d, cross_send.at[j, d], target))
        launch(slot_copy(o, d, core_send.at[0, d], mate))

    def pass_on(d):
        for j in range(1, pairs):
            s = lax.rem(pair + j, pairs) * 2 + core
            slot_copy(s, d, core_send.at[j, d], mate).wait_recv()
            launch(slot_copy(s, d, core_send.at[j, d], mate))

    spread(e)
    for step in order:
        d = peer_of(e, step, n_chan)
        send_buf[d] = relay(d)
        launch(go(step))
    for step in range(1, n_orb):
        launch(ps_copy(step))

    def pick_rows(t):
        if t == 0:
            w_copy.wait()
        base = t * tile
        own = ps_all[o][0:1, :]
        rank = lax.broadcasted_iota(jnp.int32, (tile, local), 0) + base
        hit = rank == own
        lane_block = lax.broadcasted_iota(jnp.int32, (tile, local), 1) // rows_block
        row_block[base:base + tile, :] = jnp.broadcast_to(
            jnp.sum(jnp.where(hit, lane_block, 0).astype(jnp.float32), axis=1, keepdims=True), (tile, 128)
        )
        row_size[base:base + tile, :] = jnp.broadcast_to(
            jnp.sum(jnp.where(hit, size_ref[0:1, :], 0).astype(jnp.float32), axis=1, keepdims=True), (tile, 128)
        )
        chosen = jnp.where(hit, 1.0, 0.0).astype(jnp.bfloat16)
        total = None
        for c in range(blocks):
            term = jnp.dot(
                chosen[:, c * rows_block:(c + 1) * rows_block], w_buf[c],
                preferred_element_type=jnp.float32,
            )
            total = term if total is None else total + term
        picked[base:base + tile, :] = total.astype(jnp.bfloat16)

    def mix_columns(step):
        s = lax.rem(o + step, n_orb)
        if step > 0:
            ps_wait(step)
        source = ps_all[s][0:1, :]

        def heat(t, carry):
            at = pl.ds(pl.multiple_of(t * quota, quota), quota)
            rank = lax.broadcasted_iota(jnp.int32, (quota, local), 0) + t * quota
            hot[at, :] = jnp.where(rank == source, 1.0, 0.0).astype(jnp.bfloat16)
            return carry

        lax.fori_loop(0, n_chan, heat, 0)

        def part(t, carry):
            at = pl.ds(pl.multiple_of(t * tile, tile), tile)
            mine = picked[at, pl.ds(pl.multiple_of(s * rows_block, rows_block), rows_block)].astype(jnp.float32)
            which = row_block[at, 0:1]
            lefts = [jnp.where(which == c, mine, 0.0).astype(jnp.bfloat16) for c in range(blocks)]
            for h in range(half):
                total = None
                for c in range(blocks):
                    term = lax.dot_general(
                        lefts[c],
                        hot[h * tile:(h + 1) * tile, c * rows_block:(c + 1) * rows_block],
                        (((1,), (1,)), ((), ())), preferred_element_type=jnp.float32,
                    )
                    total = term if total is None else total + term
                mix[s, h, at, :] = total.astype(jnp.bfloat16)
            return carry

        lax.fori_loop(0, rows // tile, part, 0)

    columns = 256
    span = rows // 1
    here = lax.div(e, 2)

    def slab(group, at, cols):
        z = peer_of(here, group, half)
        total = None
        for s in range(n_orb):
            term = jnp.dot(
                mix[s, z, at, :],
                recv_buf[s, pl.ds(2 * z, 2), :, cols].reshape(tile, columns),
                preferred_element_type=jnp.float32,
            )
            total = term if total is None else total + term
        return total

    def gather_group(group):
        for i in range(2):
            d = peer_of(e, 2 * group + i, n_chan)
            for j in range(pairs):
                s = lax.rem(pair + j, pairs) * 2 + (1 - core)
                slot_copy(s, d, core_send.at[j, d], mate).wait_recv()

    def add_groups(groups, fresh):
        for group in groups:
            gather_group(group)

        def block_of(t, carry):
            at = pl.ds(pl.multiple_of(lax.div(t, width // columns) * span, span), span)
            cols = pl.ds(
                pl.multiple_of(lax.rem(t, width // columns) * columns, columns), columns
            )
            total = None if fresh else total_buf[at, cols]
            for group in groups:
                term = slab(group, at, cols)
                total = term if total is None else total + term
            total_buf[at, cols] = total
            return carry

        lax.fori_loop(0, rows // span * (width // columns), block_of, 0)

    near = list(range(half // 2))
    middle = list(range(half // 2, half - 1))
    last = half - 1
    stages = {k: [] for k in range(1, n_chan)}
    stages[1] += [functools.partial(pick_rows, t) for t in range(half)]
    for s in range(n_orb):
        stages[min(2 + s, n_chan - 1)].append(functools.partial(mix_columns, s))
    stages[n_chan - 1].append(functools.partial(add_groups, near, True))
    previous = e
    for step in order:
        for piece in stages[step]:
            piece()
        d = peer_of(e, step, n_chan)
        slot_copy(o, d, core_send.at[0, d], mate).wait_recv()
        spread(d)
        pass_on(previous)
        previous = d
    if middle:
        add_groups(middle, False)
    pass_on(previous)
    gather_group(last)

    def back(d):
        return pltpu.make_async_remote_copy(
            src_ref=back_buf.at[d], dst_ref=out_ref.at[e],
            send_sem=back_send.at[d], recv_sem=back_recv.at[e],
            device_id=(d, o), device_id_type=MESH,
        )

    for g in range(half):
        first = lax.rem(lax.div(e, 2) + half // 2 + g, half) * 2
        at = pl.ds(pl.multiple_of(first * quota, tile), tile)

        def product(n, carry):
            cols = pl.ds(pl.multiple_of(n * columns, columns), columns)
            total = total_buf[at, cols] + slab(last, at, cols)
            k = lax.broadcasted_iota(jnp.int32, (tile, columns), 1) + n * columns
            rank = n_orb * lax.rem(k, rows_block) + lax.div(k, rows_block)
            kept = jnp.where(rank.astype(jnp.float32) < row_size[at, 0:1], total, 0.0)
            back_buf[pl.ds(first, 2), :, cols] = kept.astype(jnp.bfloat16).reshape(2, quota, columns)
            return carry

        lax.fori_loop(0, width // columns, product, 0)
        for i in range(2):
            if g == half // 2:
                continue
            launch(back(first + i))
        if g == half // 2:
            launch(back(peer_of(e, 1, n_chan)))
            out_ref[e] = back_buf[e]

    for step in range(1, n_chan):
        d = peer_of(e, step, n_chan)
        pltpu.make_async_remote_copy(
            src_ref=back_buf.at[d], dst_ref=out_ref.at[d],
            send_sem=back_send.at[d], recv_sem=back_recv.at[d],
            device_id=(d, o), device_id_type=MESH,
        ).wait_recv()
    for copy in started:
        copy.wait_send()


def fused(amplitudes, recoupling, interaction, pair_source, channel_sizes):
    n_chan, n_orb = lax.axis_size("chan"), lax.axis_size("orb")
    rows, width = amplitudes.shape
    quota = rows // n_chan
    blocks, rows_block = pair_source.shape
    local = blocks * rows_block
    bf16, f32 = jnp.bfloat16, jnp.float32
    vmem = pl.BlockSpec(memory_space=pltpu.VMEM)
    hbm = pl.BlockSpec(memory_space=pltpu.HBM)
    dma = pltpu.SemaphoreType.DMA
    weights = jnp.broadcast_to(recoupling[None, :], (8, rows))
    source = jnp.broadcast_to(pair_source.reshape(1, local), (8, local))
    sizes = jnp.broadcast_to(jnp.repeat(channel_sizes, rows_block)[None, :], (8, local))
    out = pl.pallas_call(
        functools.partial(kernel, n_chan, n_orb),
        out_shape=jax.ShapeDtypeStruct((n_chan, quota, width), bf16),
        in_specs=[hbm] + [vmem] * 3 + [hbm],
        out_specs=vmem,
        scratch_shapes=[
            pltpu.VMEM((rows, width), bf16),
            pltpu.VMEM((rows, 128), f32),
            pltpu.VMEM((rows, width), f32),
            pltpu.VMEM((n_chan, quota, width), bf16),
            pltpu.VMEM((n_orb, n_chan, quota, width), bf16),
            pltpu.VMEM((n_orb, 8, local), jnp.int32),
            pltpu.VMEM(interaction.shape, bf16),
            pltpu.VMEM((n_orb, n_chan // 2, rows, 2 * quota), bf16),
            pltpu.VMEM((rows, local), bf16),
            pltpu.VMEM((rows, width), bf16),
            pltpu.VMEM((rows, 128), f32),
            pltpu.VMEM((rows, 128), f32),
            pltpu.VMEM((n_chan, quota, width), bf16),
            dma,
            dma,
            dma((n_orb,)),
            dma((n_orb,)),
            dma((n_chan,)),
            dma((n_orb, n_chan)),
            dma((n_orb // 2, n_chan)),
            dma((n_orb // 2, n_chan)),
            dma((n_chan,)),
            dma((n_chan,)),
        ],
        compiler_params=pltpu.CompilerParams(
            collective_id=0, has_side_effects=True, vmem_limit_bytes=48 * 1024 * 1024
        ),
        name="cycle",
    )(amplitudes, weights, source, sizes, interaction)
    return out.reshape(rows, width)


def exchanged(amplitudes, recoupling, interaction, pair_source, return_slot, channel_sizes):
    chan_count = lax.axis_size("chan")
    orb_count = lax.axis_size("orb")
    row_count = amplitudes.shape[0]
    width = amplitudes.shape[1]
    per_peer = row_count // chan_count
    blocks_here = pair_source.shape[0]
    rows_block = pair_source.shape[1]
    relayed = (amplitudes.astype(jnp.float32) * recoupling[:, None]).astype(jnp.bfloat16)
    received = lax.all_to_all(
        relayed.reshape(chan_count, per_peer, width),
        "chan",
        split_axis=0,
        concat_axis=0,
        tiled=True,
    )
    received = received.reshape(row_count, width)
    flat_source = pair_source.reshape(-1)
    amp_rows = jnp.take(received, jnp.maximum(flat_source, 0), axis=0)
    position = jnp.arange(width, dtype=jnp.int32)
    pair_rank = orb_count * (position % rows_block) + position // rows_block
    live_mask = pair_rank[None, :] < channel_sizes[:, None]
    keep = (pair_source >= 0)[:, :, None] & live_mask[:, None, :]
    amp_block = jnp.where(
        keep, amp_rows.reshape(blocks_here, rows_block, width), jnp.zeros((), jnp.bfloat16)
    )
    cycle_local = jnp.einsum(
        "bik,bkj->bij",
        interaction,
        lax.all_gather(amp_block, "orb", axis=1, tiled=True),
        preferred_element_type=jnp.float32,
    ).astype(jnp.bfloat16)
    outgoing = jnp.take(cycle_local.reshape(blocks_here * rows_block, width), return_slot, axis=0)
    returned = lax.all_to_all(
        outgoing.reshape(chan_count, per_peer, width),
        "chan",
        split_axis=0,
        concat_axis=0,
        tiled=True,
    )
    returned = returned.reshape(row_count, width)
    return returned


def fits(amplitudes, pair_source):
    n_chan, n_orb = lax.axis_size("chan"), lax.axis_size("orb")
    rows, width = amplitudes.shape
    quota = rows // n_chan
    rows_block = pair_source.shape[1]
    return (
        quota % 16 == 0 and rows % 128 == 0 and n_chan % 4 == 0 and n_chan & (n_chan - 1) == 0
        and n_orb % 2 == 0 and rows_block % 128 == 0 and width % 256 == 0 and n_chan <= 16
    )


def shards(
    amplitudes, recoupling, denominators, interaction, pair_source, return_slot, channel_sizes
):
    if fits(amplitudes, pair_source):
        returned = fused(amplitudes, recoupling, interaction, pair_source, channel_sizes)
    else:
        returned = exchanged(
            amplitudes, recoupling, interaction, pair_source, return_slot, channel_sizes
        )
    updated = (
        amplitudes.astype(jnp.float32)
        + recoupling[:, None] * returned.astype(jnp.float32) / denominators[:, None]
    )
    return updated.astype(jnp.bfloat16)


def solution(mesh):
    in_specs = (
        P(("chan", "orb"), None),
        P(("chan", "orb")),
        P(("chan", "orb")),
        P("chan", "orb", None),
        P("chan", "orb"),
        P(("chan", "orb")),
        P("chan"),
    )
    out_specs = P(("chan", "orb"), None)
    return jax.shard_map(shards, mesh=mesh, in_specs=in_specs, out_specs=out_specs, check_vma=False)
```
